128 devices in a mesh: seq: 64 (over y, z_lo, x, core), head: 2 (over z_hi).
Axes of the slice: x: 4, y: 4, z: 4 (z_hi: 2, z_lo: 2; z = z_hi * 2 + z_lo), core: 2. Of those that a mesh axis runs over, the one named last changes fastest.
Arguments:
- tokens: bfloat16 [57344, 1024], P('seq'), may hold values from -16 to 16
- log_decay: float32 [57344, 4], P('seq', 'head'), may hold values from -1 to 0
- starts: int32 [3], replicated, may hold values from 0 to 43008, as said below
- norm1_gain: float32 [1024], replicated, may hold values from 0.1 to 1.9
- norm1_bias: float32 [1024], replicated, may hold values from -1.75 to 1.75
- query_weight: bfloat16 [1024, 1024], P(None, 'head'), may hold values from -0.1875 to 0.1875
- key_weight: bfloat16 [1024, 1024], P(None, 'head'), may hold values from -0.1875 to 0.1875
- value_weight: bfloat16 [1024, 1728], P(None, 'head'), may hold values from -0.1875 to 0.1875
- gate_weight: bfloat16 [1024, 1728], P(None, 'head'), may hold values from -0.1875 to 0.1875
- output_weight: bfloat16 [1728, 1024], P('head'), may hold values from -0.25 to 0.25
- norm2_gain: float32 [1024], replicated, may hold values from 0.1 to 1.9
- norm2_bias: float32 [1024], replicated, may hold values from -1.75 to 1.75
- ffn_gate: bfloat16 [1024, 1728], P(None, 'head'), may hold values from -0.1875 to 0.1875
- ffn_up: bfloat16 [1024, 1728], P(None, 'head'), may hold values from -0.1875 to 0.1875
- ffn_down: bfloat16 [1728, 1024], P('head'), may hold values from -0.21875 to 0.21875
- cotangent: bfloat16 [57344, 1024], P('seq', 'head'), may hold values from -16 to 16
Outputs:
- output: bfloat16 [57344, 1024], P('seq', 'head')
- input_grad: bfloat16 [57344, 1024], P('seq', 'head')
- norm1_gain_grad: float32 [1024], P('seq')
- norm1_bias_grad: float32 [1024], P('seq')
- query_weight_grad: float32 [1024, 1024], P('seq', 'head')
- key_weight_grad: float32 [1024, 1024], P('seq', 'head')
- value_weight_grad: float32 [1024, 1728], P('seq', 'head')
- gate_weight_grad: float32 [1024, 1728], P('seq', 'head')
- output_weight_grad: float32 [1728, 1024], P('head', 'seq')
- norm2_gain_grad: float32 [1024], P('seq')
- norm2_bias_grad: float32 [1024], P('seq')
- ffn_gate_grad: float32 [1024, 1728], P('seq', 'head')
- ffn_up_grad: float32 [1024, 1728], P('seq', 'head')
- ffn_down_grad: float32 [1728, 1024], P('head', 'seq')
The draws below stay inside these ranges and needn't reach their ends.
Inputs may be any that keep to these rules, and one draw needn't show every extreme that they name: starts[0] = 0 and the offsets rise strictly; every document has 14336 tokens or more; the last document starts at 43008.
All inputs are finite; a program needn't handle non-finite values.
Results may differ from the reference program's by a relative error of at most 0.035.
Values may be sent and summed in bfloat16 or wider, within the bound.
No kernel may reach another device: no remote copies, remote signals or barrier semaphores. Data moves between devices by JAX's collectives and lax.ppermute only.
A program may use at most 256 MiB of HBM per device.

```python
import math
import jax
import jax.numpy as jnp
from jax import lax

D = 1024
RETENTION_HEADS = 4
DV = 432
FF = 1728
DK = 256
VD = 1728
TOK_DEV = 896
TOKEN_TOTAL = 57344


def draw_starts(key, part):
    key = jax.random.fold_in(key, 11)
    least_gap = TOKEN_TOTAL // 4
    second = jax.random.randint(key, (), least_gap, TOKEN_TOTAL - 2 * least_gap + 1)
    third = jnp.full((), TOKEN_TOTAL - least_gap, jnp.int32)
    return jnp.stack([jnp.zeros((), jnp.int32), second.astype(jnp.int32), third])


def draw_log_decay(key, part):
    key = jax.random.fold_in(key, 23)
    random_subkeys = jax.random.split(key, 7)
    fast_count = RETENTION_HEADS // 2
    ranking = jax.random.permutation(random_subkeys[0], RETENTION_HEADS)
    fast_heads = ranking < fast_count
    fast_rate = jnp.exp(jax.random.uniform(random_subkeys[1], (RETENTION_HEADS,), minval=math.log(1.0 / 50.0), maxval=math.log(1.0 / 30.0)))
    slow_rate = jnp.exp(jax.random.uniform(random_subkeys[2], (RETENTION_HEADS,), minval=math.log(0.1), maxval=math.log(0.6))) / TOKEN_TOTAL
    decay_rates_full = jnp.where(fast_heads, fast_rate, slow_rate)
    segment_factor = jnp.exp(jax.random.uniform(random_subkeys[3], (TOKEN_TOTAL // 64 + 1, RETENTION_HEADS), minval=math.log(0.5), maxval=math.log(2.0)))
    segment_factor = jnp.repeat(segment_factor, 64, axis=0)[:TOKEN_TOTAL]
    coarse_factor = jnp.exp(jax.random.uniform(random_subkeys[4], (TOKEN_TOTAL, RETENTION_HEADS), minval=math.log(0.7), maxval=math.log(1.4)))
    segment_begin = jax.random.uniform(random_subkeys[5], (TOKEN_TOTAL, RETENTION_HEADS)) < 2.0 / TOKEN_TOTAL
    segment_length = jnp.log(jax.random.uniform(random_subkeys[6], (TOKEN_TOTAL, RETENTION_HEADS), minval=0.5, maxval=0.8))
    return (-(decay_rates_full[None, :] * segment_factor * coarse_factor) + jnp.where(segment_begin, segment_length, 0.0)).astype(jnp.float32)


def with_spikes(values, stream_key, source, target, shards_of, factor):
    def block_of(dim):
        return (jnp.arange(values.shape[dim]) // (values.shape[dim] // shards_of)).reshape((-1,) + (1,) * (values.ndim - 1 - dim))

    near = jax.random.permutation(stream_key, shards_of)[block_of(target)]
    far = (block_of(target) + shards_of // 2) % shards_of
    return jnp.where((block_of(source) == near) | (block_of(source) == far), factor * values, values)


def levels(stream_key, dims, cuts, smallest, largest):
    loudness = 1.0
    for position, parts in cuts:
        heights = jax.random.uniform(jax.random.fold_in(jax.random.fold_in(stream_key, 6), position), (parts,), jnp.float32, smallest / len(cuts), largest / len(cuts))
        loudness = loudness * jnp.repeat(jnp.exp(heights), dims[position] // parts).reshape((-1,) + (1,) * (len(dims) - 1 - position))
    return loudness


def gaussian(stream_key, extent, scale, limit, shards=(), kind=jnp.bfloat16):
    entries = jax.random.normal(stream_key, extent, jnp.float32) * scale
    if len(shards) > 0:
        entries = levels(stream_key, extent, shards, -0.22, 0.18) * entries
    return jnp.clip(entries, min=-limit, max=limit).astype(kind)


def bell_draw_with(stream_key, shape, width, bound, pieces, heavy, held_as=jnp.bfloat16):
    values = width * jax.random.normal(stream_key, shape, jnp.float32)
    if pieces:
        values = values * levels(stream_key, shape, pieces, -0.22, 0.18)
    return jnp.clip(with_spikes(values, jax.random.fold_in(stream_key, 3), *heavy), -bound, bound).astype(held_as)


def setup_inputs(seed: int = 0) -> dict:
    seeds = jax.random.split(jax.random.key(seed), 17)
    return {
        "tokens": bell_draw_with(seeds[0], (TOKEN_TOTAL, D), 1.0, 16.0, ((0, 64),), (0, 1, 64, 4.0)),
        "log_decay": draw_log_decay(jax.random.fold_in(seeds[16], 71), 0),
        "starts": draw_starts(jax.random.fold_in(seeds[16], 71), 0),
        "norm1_gain": jnp.clip(1.0 + 0.18 * jax.random.normal(seeds[3], (D,), jnp.float32), 0.1, 1.9),
        "norm1_bias": gaussian(seeds[4], (D,), 0.3, 1.75, (), jnp.float32),
        "query_weight": gaussian(seeds[5], (D, D), D ** -0.5, 0.1875, ((1, 2),)),
        "key_weight": gaussian(seeds[6], (D, D), D ** -0.5, 0.1875, ((1, 2),)),
        "value_weight": gaussian(seeds[7], (D, VD), D ** -0.5, 0.1875, ((1, 2),)),
        "gate_weight": gaussian(seeds[8], (D, VD), D ** -0.5, 0.1875, ((1, 2),)),
        "output_weight": gaussian(seeds[9], (VD, D), (VD // 3) ** -0.5, 0.25, ((0, 2),)),
        "norm2_gain": jnp.clip(1.0 + 0.18 * jax.random.normal(seeds[10], (D,), jnp.float32), 0.1, 1.9),
        "norm2_bias": gaussian(seeds[11], (D,), 0.3, 1.75, (), jnp.float32),
        "ffn_gate": gaussian(seeds[12], (D, FF), D ** -0.5, 0.1875, ((1, 2),)),
        "ffn_up": gaussian(seeds[13], (D, FF), D ** -0.5, 0.1875, ((1, 2),)),
        "ffn_down": gaussian(seeds[14], (FF, D), (FF // 2) ** -0.5, 0.21875, ((0, 2),)),
        "cotangent": bell_draw_with(seeds[15], (TOKEN_TOTAL, D), 1.0, 16.0, ((0, 64), (1, 2)), (0, 1, 64, 4.0)),
    }


@jax.custom_vjp
def low(v):
    return lax.optimization_barrier(v.astype(jnp.bfloat16)).astype(jnp.float32)

@jax.custom_vjp
def low_back(v):
    return v

def low_keep(v):
    return (low(v), None)

def low_pass(kept, grad):
    return (grad,)

def back_keep(v):
    return (v, None)

def back_low(kept, grad):
    return (low(grad),)
low.defvjp(low_keep, low_pass)
low_back.defvjp(back_keep, back_low)
eps_norm = 1e-05
maximal_precision = lax.Precision.HIGHEST

def layer_norm(values, gain_vec, bias_vec):
    average = lax.optimization_barrier(jnp.mean(values, axis=-1, keepdims=True))
    centred = values - average
    variance = lax.optimization_barrier(jnp.mean(centred * centred, axis=-1, keepdims=True))
    return centred * lax.rsqrt(variance + eps_norm) * gain_vec + bias_vec

def group_norm(values):
    average = lax.optimization_barrier(jnp.mean(values, axis=-1, keepdims=True))
    centred = values - average
    variance = lax.optimization_barrier(jnp.mean(centred * centred, axis=-1, keepdims=True))
    return centred * lax.rsqrt(variance + eps_norm)

def rotary_angles(positions, key_size):
    half_size = key_size // 2
    frequency = jnp.exp(-math.log(10000.0) * jnp.arange(half_size, dtype=jnp.float32) / half_size)
    return positions.astype(jnp.float32)[:, None] * frequency[None, :]

def rotate(vectors, angles):
    half_size = vectors.shape[-1] // 2
    upper_half = vectors[..., :half_size]
    lower_half = vectors[..., half_size:]
    cosine = jnp.cos(angles)[:, None, :]
    sine_part = jnp.sin(angles)[:, None, :]
    return jnp.concatenate([upper_half * cosine - lower_half * sine_part, lower_half * cosine + upper_half * sine_part], axis=-1)

def links(starts, positions, block_start):
    started = starts[None, :] <= positions[:, None]
    doc_ids = lax.optimization_barrier(jnp.sum(started.astype(jnp.int32), axis=1))
    inside = jnp.logical_and(starts[None, :] >= block_start, started)
    opened = lax.optimization_barrier(jnp.sum(inside.astype(jnp.int32), axis=1)) == 0
    tail_same = doc_ids == doc_ids[-1]
    causal = positions[:, None] >= positions[None, :]
    allowed = jnp.logical_and(causal, doc_ids[:, None] == doc_ids[None, :])
    return (opened, tail_same, allowed)

def decay_terms(log_decay, opened, tail_same, allowed):
    climb_sum = jnp.cumsum(log_decay, axis=0)
    climb_heads = climb_sum.T
    spread = climb_heads[:, :, None] - climb_heads[:, None, :]
    decay_mask = jnp.where(allowed[None, :, :], jnp.exp(jnp.minimum(spread, 0.0)), 0.0)
    entering_weight = jnp.where(opened[:, None], jnp.exp(climb_sum), 0.0)
    exiting_weight = jnp.where(tail_same[:, None], jnp.exp(climb_sum[-1][None, :] - climb_sum), 0.0)
    carry_decay = entering_weight[-1]
    return (decay_mask, entering_weight, exiting_weight, carry_decay)

def retention(query_rot, key_rot, values, log_decay, starts):
    blocks = TOKEN_TOTAL // TOK_DEV

    def shaped(array):
        return array.reshape((blocks, TOK_DEV) + array.shape[1:])
    offsets = jnp.arange(blocks, dtype=jnp.int32) * TOK_DEV

    @jax.checkpoint
    def block_step(current_state, inputs):
        query_rows, key_matrix, value_matrix, decay_rows, block_start = inputs
        positions = block_start + jnp.arange(TOK_DEV, dtype=jnp.int32)
        opened, tail_same, allowed = links(starts, positions, block_start)
        decay_mask, entering_weight, exiting_weight, carry_decay = decay_terms(decay_rows, opened, tail_same, allowed)
        scores = low_back(jnp.einsum('thk,shk->hts', query_rows, key_matrix, precision=maximal_precision))
        weights = low(scores * decay_mask)
        retention_output = jnp.einsum('hts,shv->thv', weights, value_matrix, precision=maximal_precision)
        retention_output = retention_output + jnp.einsum('wrj,rjd->wrd', query_rows * entering_weight[:, :, None], current_state, precision=maximal_precision)
        segment_state = jnp.einsum('zbe,zbc->bec', key_matrix * exiting_weight[:, :, None], value_matrix, precision=maximal_precision)
        return (carry_decay[:, None, None] * current_state + segment_state, retention_output)
    zero_state = jnp.zeros((RETENTION_HEADS, DK, DV), jnp.float32)
    final_state, retention_output = lax.scan(block_step, zero_state, (shaped(query_rot), shaped(key_rot), shaped(values), shaped(log_decay), offsets))
    return retention_output.reshape(TOKEN_TOTAL, RETENTION_HEADS, DV)

def reference(tokens, log_decay, starts, norm1_gain, norm1_bias, query_weight, key_weight, value_weight, gate_weight, output_weight, norm2_gain, norm2_bias, ffn_gate, ffn_up, ffn_down, cotangent):
    angles = rotary_angles(jnp.arange(TOKEN_TOTAL, dtype=jnp.int32), DK)

    def forward(inputs, gain_one, bias_one, w_query, w_key, w_value, w_gate, w_output, gain_two, bias_two, w_ffn_gate, w_ffn_up, w_ffn_down):
        normed1 = low(layer_norm(inputs, gain_one, bias_one))
        query_rows = low_back(jnp.dot(normed1, w_query, precision=maximal_precision))
        key_matrix = low_back(jnp.dot(normed1, w_key, precision=maximal_precision))
        values = low(low_back(jnp.dot(normed1, w_value, precision=maximal_precision)))
        gate_act = low_back(jnp.dot(normed1, w_gate, precision=maximal_precision))
        query_rot = low(rotate(query_rows.reshape(TOKEN_TOTAL, RETENTION_HEADS, DK), angles))
        key_rot = low(rotate(key_matrix.reshape(TOKEN_TOTAL, RETENTION_HEADS, DK), angles) * DK ** (-0.5))
        retention_output = low_back(retention(query_rot, key_rot, values.reshape(TOKEN_TOTAL, RETENTION_HEADS, DV), log_decay, starts))
        mixed = low(jax.nn.silu(gate_act) * group_norm(retention_output).reshape(TOKEN_TOTAL, VD))
        branch = low_back(jnp.dot(mixed, w_output, precision=maximal_precision))
        resid = inputs + branch
        normed2 = low(layer_norm(resid, gain_two, bias_two))
        gate_ff = low_back(jnp.dot(normed2, w_ffn_gate, precision=maximal_precision))
        up_ff = low_back(jnp.dot(normed2, w_ffn_up, precision=maximal_precision))
        hidden = low(jax.nn.gelu(gate_ff, approximate=False) * up_ff)
        return resid + low_back(jnp.dot(hidden, w_ffn_down, precision=maximal_precision))
    params = (tokens.astype(jnp.float32), norm1_gain, norm1_bias, query_weight.astype(jnp.float32), key_weight.astype(jnp.float32), value_weight.astype(jnp.float32), gate_weight.astype(jnp.float32), output_weight.astype(jnp.float32), norm2_gain, norm2_bias, ffn_gate.astype(jnp.float32), ffn_up.astype(jnp.float32), ffn_down.astype(jnp.float32))
    result, backward = jax.vjp(forward, *params)
    gradients = backward(cotangent.astype(jnp.float32))
    return (result.astype(jnp.bfloat16), gradients[0].astype(jnp.bfloat16), gradients[1], gradients[2], gradients[3], gradients[4], gradients[5], gradients[6], gradients[7], gradients[8], gradients[9], gradients[10], gradients[11], gradients[12])
```

```python
import math

import jax
import jax.numpy as jnp
from jax import lax
from jax.sharding import Mesh, PartitionSpec as P

eps_norm = 1e-05
bf16 = jnp.bfloat16
f32 = jnp.float32
SEQ = ("y", "zlo", "x", "core")
CHIPS = ("y", "zlo", "x")
HEAD = "zhi"
SWAP = [(0, 1), (1, 0)]


def dot(left, right):
    return lax.dot_general(left, right, (((1,), (0,)), ((), ())), preferred_element_type=f32)


def token_sum(left, right):
    return lax.dot_general(left, right, (((0,), (0,)), ((), ())), preferred_element_type=f32)


def row_times(left, right):
    return lax.dot_general(left, right, (((1,), (1,)), ((), ())), preferred_element_type=f32)


def norm_stats(values):
    average = jnp.mean(values, axis=-1, keepdims=True)
    centred = values - average
    variance = jnp.mean(centred * centred, axis=-1, keepdims=True)
    inverse = lax.rsqrt(variance + eps_norm)
    return centred * inverse, inverse


def norm_back(xhat, inverse, grad):
    first = jnp.mean(grad, axis=-1, keepdims=True)
    second = jnp.mean(grad * xhat, axis=-1, keepdims=True)
    return inverse * (grad - first - xhat * second)


def swap_heads(array):
    return lax.ppermute(array, HEAD, SWAP)


def rotate(vectors, cosine, sine):
    upper, lower = vectors[:, : cosine.shape[1]], vectors[:, cosine.shape[1] :]
    return jnp.concatenate([upper * cosine - lower * sine, lower * cosine + upper * sine], axis=1)


def split3(values):
    first = values.astype(bf16)
    rest = values - first.astype(f32)
    second = rest.astype(bf16)
    third = (rest - second.astype(f32)).astype(bf16)
    return first, second, third


def block_weights(log_totals, starts, row_count, head):
    blocks = log_totals.shape[0]
    begin = jnp.arange(blocks, dtype=jnp.int32) * row_count
    has_start = jnp.any(
        (starts[None, :] >= begin[:, None]) & (starts[None, :] < begin[:, None] + row_count), axis=1
    )
    own = jnp.where(head == 0, log_totals[:, 0], log_totals[:, 1])
    index = jnp.arange(blocks, dtype=jnp.int32)
    inner = (index[None, :, None] < index[None, None, :]) & (
        index[None, None, :] < index[:, None, None]
    )
    logs = jnp.sum(jnp.where(inner, own[None, None, :], 0.0), axis=2)
    broken = jnp.any(inner & has_start[None, None, :], axis=2)
    later = index[:, None] > index[None, :]
    return jnp.where(later & ~broken, jnp.exp(logs), 0.0)


def local(
    tokens,
    log_decay,
    starts,
    norm1_gain,
    norm1_bias,
    query_weight,
    key_weight,
    value_weight,
    gate_weight,
    output_weight,
    norm2_gain,
    norm2_bias,
    ffn_gate,
    ffn_up,
    ffn_down,
    cotangent,
):
    rows, width = tokens.shape
    heads = log_decay.shape[1]
    dk = query_weight.shape[1] // heads
    dv = value_weight.shape[1] // heads
    half = width // 2
    blocks = lax.axis_size(SEQ)
    seq_at = lax.axis_index(SEQ)
    head_at = lax.axis_index(HEAD)
    core_at = lax.axis_index("core")
    first_head = head_at == 0
    block_start = seq_at * rows
    key_scale = dk ** (-0.5)

    other_cot = swap_heads(cotangent)

    positions = block_start + jnp.arange(rows, dtype=jnp.int32)
    started = starts[None, :] <= positions[:, None]
    doc_ids = jnp.sum(started.astype(jnp.int32), axis=1)
    inside = jnp.logical_and(starts[None, :] >= block_start, started)
    opened = jnp.sum(inside.astype(jnp.int32), axis=1) == 0
    tail_same = doc_ids == doc_ids[-1]
    allowed = (positions[:, None] >= positions[None, :]) & (doc_ids[:, None] == doc_ids[None, :])
    climb = jnp.cumsum(log_decay, axis=0)
    climb_rows = climb.T
    total = climb[-1]
    entering = jnp.where(opened[:, None], jnp.exp(climb), 0.0)
    leaving = jnp.where(tail_same[:, None], jnp.exp(total[None, :] - climb), 0.0)
    masks = [
        jnp.where(
            allowed,
            jnp.exp(jnp.minimum(climb[:, h : h + 1] - climb_rows[h : h + 1, :], 0.0)),
            0.0,
        )
        for h in range(heads)
    ]
    frequency = jnp.exp(-math.log(10000.0) * jnp.arange(dk // 2, dtype=f32) / (dk // 2))
    angles = positions.astype(f32)[:, None] * frequency[None, :]
    cosine, sine = jnp.cos(angles), jnp.sin(angles)

    wide = tokens.astype(f32)
    xhat1, inverse1 = norm_stats(wide)
    normed1 = (xhat1 * norm1_gain + norm1_bias).astype(bf16)
    keys, values, queries, gates, exits = [], [], [], [], []
    value_parts = [value_weight[:, h * dv : (h + 1) * dv] for h in range(heads)]
    gate_parts = [gate_weight[:, h * dv : (h + 1) * dv] for h in range(heads)]
    for h in range(heads):
        rows_k = dot(normed1, key_weight[:, h * dk : (h + 1) * dk])
        key = (rotate(rows_k, cosine, sine) * key_scale).astype(bf16)
        keys.append(key)
        values.append(dot(normed1, value_parts[h]).astype(bf16))
        exits.append((key.astype(f32) * leaving[:, h : h + 1]).astype(bf16))
    states = jnp.concatenate([token_sum(exits[h], values[h]) for h in range(heads)], axis=0)
    pieces = states.astype(bf16).reshape(blocks, heads * dk // blocks, dv)
    marks = jnp.concatenate([part for part in split3(total)])
    marks = jnp.broadcast_to(
        jnp.pad(marks, (0, 128 - 3 * heads - dv % 128))[None, None, :],
        (blocks, pieces.shape[1], 128 - dv % 128),
    )
    arrived = lax.all_to_all(jnp.concatenate([pieces, marks], axis=2), SEQ, 0, 0, tiled=True)
    tags = arrived[:, 0, dv : dv + 3 * heads].astype(f32)
    log_totals = tags[:, :heads] + tags[:, heads : 2 * heads] + tags[:, 2 * heads :]
    piece_head = seq_at // (blocks // heads)
    carried = block_weights(log_totals, starts, rows, piece_head).astype(bf16)
    summed = lax.dot_general(
        carried, arrived[:, :, :dv], (((1,), (0,)), ((), ())), preferred_element_type=f32
    ).astype(bf16)
    incoming = lax.all_to_all(summed, SEQ, 0, 0, tiled=True).reshape(heads * dk, dv)

    mixed, ghats, ginvs, weights = [], [], [], []
    branch = None
    output_parts = [output_weight[h * dv : (h + 1) * dv] for h in range(heads)]
    for h in range(heads):
        rows_q = dot(normed1, query_weight[:, h * dk : (h + 1) * dk])
        query = rotate(rows_q, cosine, sine).astype(bf16)
        queries.append(query)
        gates.append(dot(normed1, gate_parts[h]))
        weight = (row_times(query, keys[h]) * masks[h]).astype(bf16)
        weights.append(weight)
        retained = dot(weight, values[h])
        retained = retained + entering[:, h : h + 1] * dot(query, incoming[h * dk : (h + 1) * dk])
        ghat, ginv = norm_stats(retained)
        ghats.append(ghat)
        ginvs.append(ginv)
        mix = (jax.nn.silu(gates[h]) * ghat).astype(bf16)
        mixed.append(mix)
        part = dot(mix, output_parts[h])
        branch = part if branch is None else branch + part
    branch = branch.astype(bf16)
    resid = wide + branch.astype(f32) + swap_heads(branch).astype(f32)

    xhat2, inverse2 = norm_stats(resid)
    normed2 = (xhat2 * norm2_gain + norm2_bias).astype(bf16)
    gate_ff = dot(normed2, ffn_gate)
    up_ff = dot(normed2, ffn_up)
    cdf = 0.5 * (1.0 + lax.erf(gate_ff * (0.5**0.5)))
    gelu = gate_ff * cdf
    hidden = (gelu * up_ff).astype(bf16)
    ffn_out = dot(hidden, ffn_down).astype(bf16)
    low, high = ffn_out[:, :half], ffn_out[:, half:]
    arrived_out = swap_heads(jnp.where(first_head, high, low))
    own_resid = jnp.where(first_head, resid[:, :half], resid[:, half:])
    output = (
        own_resid + (jnp.where(first_head, low, high).astype(f32) + arrived_out.astype(f32))
    ).astype(bf16)

    cot = jnp.concatenate(
        [
            jnp.where(first_head, cotangent, other_cot),
            jnp.where(first_head, other_cot, cotangent),
        ],
        axis=1,
    )
    hidden_grad = row_times(cot, ffn_down)
    pdf = (1.0 / math.sqrt(2.0 * math.pi)) * jnp.exp(-0.5 * gate_ff * gate_ff)
    gate_ff_grad = (hidden_grad * up_ff * (cdf + gate_ff * pdf)).astype(bf16)
    up_ff_grad = (hidden_grad * gelu).astype(bf16)
    normed2_part = (row_times(gate_ff_grad, ffn_gate) + row_times(up_ff_grad, ffn_up)).astype(bf16)
    normed2_grad = normed2_part.astype(f32) + swap_heads(normed2_part).astype(f32)
    gain2_grad = jnp.sum(normed2_grad * xhat2, axis=0)
    bias2_grad = jnp.sum(normed2_grad, axis=0)
    resid_grad = cot.astype(f32) + norm_back(xhat2, inverse2, normed2_grad * norm2_gain)
    branch_grad = resid_grad.astype(bf16)

    gate_grads, retained_grads, state_parts = [], [], []
    for h in range(heads):
        mixed_grad = row_times(branch_grad, output_parts[h])
        sig = jax.nn.sigmoid(gates[h])
        gate_grads.append(
            (mixed_grad * ghats[h] * (sig * (1.0 + gates[h] * (1.0 - sig)))).astype(bf16)
        )
        retained_grad = norm_back(ghats[h], ginvs[h], mixed_grad * (gates[h] * sig)).astype(bf16)
        retained_grads.append(retained_grad)
        scaled = (queries[h].astype(f32) * entering[:, h : h + 1]).astype(bf16)
        state_parts.append(token_sum(scaled, retained_grad))
    pieces = jnp.concatenate(state_parts, axis=0).astype(bf16)
    pieces = pieces.reshape(blocks, heads * dk // blocks, dv)
    arrived_back = lax.all_to_all(pieces, SEQ, 0, 0, tiled=True)
    summed_back = lax.dot_general(
        carried, arrived_back, (((0,), (0,)), ((), ())), preferred_element_type=f32
    ).astype(bf16)
    outgoing = lax.all_to_all(summed_back, SEQ, 0, 0, tiled=True).reshape(heads * dk, dv)

    query_grads, key_grads, value_grads = [], [], []
    for h in range(heads):
        rg = retained_grads[h]
        out_state = outgoing[h * dk : (h + 1) * dk]
        in_state = incoming[h * dk : (h + 1) * dk]
        score_grad = (row_times(rg, values[h]) * masks[h]).astype(bf16)
        query_rot = dot(score_grad, keys[h]) + entering[:, h : h + 1] * row_times(rg, in_state)
        key_rot = token_sum(score_grad, queries[h]) + leaving[:, h : h + 1] * row_times(
            values[h], out_state
        )
        value_grad = token_sum(weights[h], rg) + leaving[:, h : h + 1] * dot(keys[h], out_state)
        query_grads.append(rotate(query_rot, cosine, -sine).astype(bf16))
        key_grads.append((rotate(key_rot, cosine, -sine) * key_scale).astype(bf16))
        value_grads.append(value_grad.astype(bf16))
    normed1_part = None
    for h in range(heads):
        for grad, weight in (
            (query_grads[h], query_weight[:, h * dk : (h + 1) * dk]),
            (key_grads[h], key_weight[:, h * dk : (h + 1) * dk]),
            (value_grads[h], value_parts[h]),
            (gate_grads[h], gate_parts[h]),
        ):
            part = row_times(grad, weight)
            normed1_part = part if normed1_part is None else normed1_part + part
    normed1_part = normed1_part.astype(bf16)
    low, high = normed1_part[:, :half], normed1_part[:, half:]
    arrived_grad = swap_heads(jnp.where(first_head, high, low))
    normed1_grad = jnp.where(first_head, low, high).astype(f32) + arrived_grad.astype(f32)
    own_hat = jnp.where(first_head, xhat1[:, :half], xhat1[:, half:])
    own_gain = jnp.where(first_head, norm1_gain[:half], norm1_gain[half:])
    scaled_grad = normed1_grad * own_gain
    sums = jnp.stack([jnp.sum(scaled_grad, axis=1), jnp.sum(scaled_grad * own_hat, axis=1)])
    sums = (sums + swap_heads(sums)) * (1.0 / width)
    own_back = inverse1 * (scaled_grad - sums[0][:, None] - own_hat * sums[1][:, None])
    own_resid_grad = jnp.where(first_head, resid_grad[:, :half], resid_grad[:, half:])
    input_grad = (own_resid_grad + own_back).astype(bf16)
    own_norm1 = jnp.stack([jnp.sum(normed1_grad * own_hat, axis=0), jnp.sum(normed1_grad, axis=0)])
    other_norm1 = swap_heads(own_norm1)
    norm1_grads = jnp.concatenate(
        [
            jnp.where(first_head, own_norm1, other_norm1),
            jnp.where(first_head, other_norm1, own_norm1),
        ],
        axis=1,
    )
    vectors = jnp.concatenate([norm1_grads, gain2_grad[None], bias2_grad[None]], axis=0)
    vector_high = vectors.astype(bf16)
    vector_low = (vectors - vector_high.astype(f32)).astype(bf16)

    grads = [token_sum(normed1, query_grads[h]).astype(bf16) for h in range(heads)]
    grads += [token_sum(normed1, key_grads[h]).astype(bf16) for h in range(heads)]
    grads += [token_sum(normed1, value_grads[h]).astype(bf16) for h in range(heads)]
    grads += [token_sum(normed1, gate_grads[h]).astype(bf16) for h in range(heads)]
    grads += [token_sum(branch_grad, mixed[h]).astype(bf16) for h in range(heads)]
    grads += [token_sum(normed2, gate_ff_grad).astype(bf16)]
    grads += [token_sum(normed2, up_ff_grad).astype(bf16)]
    grads += [token_sum(cot, hidden).astype(bf16)]
    grads += [vector_high.T, vector_low.T]
    widths = [g.shape[1] for g in grads]
    everything = jnp.concatenate(grads, axis=1)
    everything = everything.reshape(blocks // 2, 2, width // blocks, -1)
    kept = jnp.where(core_at == 0, everything[:, 0], everything[:, 1])
    sent = jnp.where(core_at == 0, everything[:, 1], everything[:, 0])
    got = lax.ppermute(sent, "core", SWAP)
    chip_sum = (kept.astype(f32) + got.astype(f32)).astype(bf16)
    shares = lax.all_to_all(chip_sum, CHIPS, 0, 0, tiled=True)
    whole = jnp.sum(shares.astype(f32), axis=0)
    parts, at = [], 0
    for wide_part in widths:
        parts.append(whole[:, at : at + wide_part])
        at += wide_part
    query_out = jnp.concatenate(parts[0:2], axis=1)
    key_out = jnp.concatenate(parts[2:4], axis=1)
    value_out = jnp.concatenate(parts[4:6], axis=1)
    gate_out = jnp.concatenate(parts[6:8], axis=1)
    output_out = jnp.concatenate(parts[8:10], axis=1).T
    ffn_gate_out, ffn_up_out, ffn_down_out = parts[10], parts[11], parts[12].T
    vector_out = parts[13] + parts[14]
    return (
        output,
        input_grad,
        vector_out[:, 0],
        vector_out[:, 1],
        query_out,
        key_out,
        value_out,
        gate_out,
        output_out,
        vector_out[:, 2],
        vector_out[:, 3],
        ffn_gate_out,
        ffn_up_out,
        ffn_down_out,
    )


def solution(mesh):
    fine = Mesh(mesh.devices.reshape(4, 2, 4, 2, 2), SEQ + (HEAD,))
    return jax.shard_map(
        local,
        mesh=fine,
        in_specs=(
            P(SEQ, None),
            P(SEQ, HEAD),
            P(),
            P(),
            P(),
            P(None, HEAD),
            P(None, HEAD),
            P(None, HEAD),
            P(None, HEAD),
            P(HEAD, None),
            P(),
            P(),
            P(None, HEAD),
            P(None, HEAD),
            P(HEAD, None),
            P(SEQ, HEAD),
        ),
        out_specs=(
            P(SEQ, HEAD),
            P(SEQ, HEAD),
            P(SEQ),
            P(SEQ),
            P(SEQ, HEAD),
            P(SEQ, HEAD),
            P(SEQ, HEAD),
            P(SEQ, HEAD),
            P(HEAD, SEQ),
            P(SEQ),
            P(SEQ),
            P(SEQ, HEAD),
            P(SEQ, HEAD),
            P(HEAD, SEQ),
        ),
        check_vma=False,
    )
```

```python
import math

import jax
import jax.numpy as jnp
from jax import lax
from jax.sharding import Mesh, PartitionSpec as P

eps_norm = 1e-05
bf16 = jnp.bfloat16
f32 = jnp.float32
SEQ = ("y", "zlo", "x", "core")
CHIPS = ("y", "zlo", "x")
HEAD = "zhi"
SWAP = [(0, 1), (1, 0)]


def dot(left, right):
    return lax.dot_general(left, right, (((1,), (0,)), ((), ())), preferred_element_type=f32)


def token_sum(left, right):
    return lax.dot_general(left, right, (((0,), (0,)), ((), ())), preferred_element_type=f32)


def row_times(left, right):
    return lax.dot_general(left, right, (((1,), (1,)), ((), ())), preferred_element_type=f32)


def norm_stats(values):
    average = jnp.mean(values, axis=-1, keepdims=True)
    centred = values - average
    variance = jnp.mean(centred * centred, axis=-1, keepdims=True)
    inverse = lax.rsqrt(variance + eps_norm)
    return centred * inverse, inverse


def norm_back(xhat, inverse, grad):
    first = jnp.mean(grad, axis=-1, keepdims=True)
    second = jnp.mean(grad * xhat, axis=-1, keepdims=True)
    return inverse * (grad - first - xhat * second)


def swap_heads(array):
    return lax.ppermute(array, HEAD, SWAP)


def rotate(vectors, cosine, sine):
    upper, lower = vectors[:, : cosine.shape[1]], vectors[:, cosine.shape[1] :]
    return jnp.concatenate([upper * cosine - lower * sine, lower * cosine + upper * sine], axis=1)


def split3(values):
    first = values.astype(bf16)
    rest = values - first.astype(f32)
    second = rest.astype(bf16)
    third = (rest - second.astype(f32)).astype(bf16)
    return first, second, third


def exchange_sum(grads):
    blocks = lax.axis_size(SEQ)
    rows = grads[0].shape[0] // blocks
    stacked = jnp.concatenate([g.astype(bf16).reshape(blocks, 1, rows, -1) for g in grads], axis=1)
    stacked = stacked.reshape(blocks, len(grads) * rows, -1)
    shares = lax.all_to_all(stacked, SEQ, 0, 0, tiled=True)
    total = jnp.sum(shares.astype(f32), axis=0)
    return jnp.swapaxes(total.reshape(len(grads), rows, -1), 0, 1)


def block_weights(log_totals, starts, row_count, head):
    blocks = log_totals.shape[0]
    begin = jnp.arange(blocks, dtype=jnp.int32) * row_count
    has_start = jnp.any(
        (starts[None, :] >= begin[:, None]) & (starts[None, :] < begin[:, None] + row_count), axis=1
    )
    own = jnp.where(head == 0, log_totals[:, 0], log_totals[:, 1])
    index = jnp.arange(blocks, dtype=jnp.int32)
    inner = (index[None, :, None] < index[None, None, :]) & (
        index[None, None, :] < index[:, None, None]
    )
    logs = jnp.sum(jnp.where(inner, own[None, None, :], 0.0), axis=2)
    broken = jnp.any(inner & has_start[None, None, :], axis=2)
    later = index[:, None] > index[None, :]
    return jnp.where(later & ~broken, jnp.exp(logs), 0.0)


def local(
    tokens,
    log_decay,
    starts,
    norm1_gain,
    norm1_bias,
    query_weight,
    key_weight,
    value_weight,
    gate_weight,
    output_weight,
    norm2_gain,
    norm2_bias,
    ffn_gate,
    ffn_up,
    ffn_down,
    cotangent,
):
    rows, width = tokens.shape
    heads = log_decay.shape[1]
    dk = query_weight.shape[1] // heads
    dv = value_weight.shape[1] // heads
    half = width // 2
    blocks = lax.axis_size(SEQ)
    seq_at = lax.axis_index(SEQ)
    head_at = lax.axis_index(HEAD)
    first_head = head_at == 0
    block_start = seq_at * rows
    key_scale = dk ** (-0.5)

    other_cot = swap_heads(cotangent)

    positions = block_start + jnp.arange(rows, dtype=jnp.int32)
    started = starts[None, :] <= positions[:, None]
    doc_ids = jnp.sum(started.astype(jnp.int32), axis=1)
    inside = jnp.logical_and(starts[None, :] >= block_start, started)
    opened = jnp.sum(inside.astype(jnp.int32), axis=1) == 0
    tail_same = doc_ids == doc_ids[-1]
    allowed = (positions[:, None] >= positions[None, :]) & (doc_ids[:, None] == doc_ids[None, :])
    climb = jnp.cumsum(log_decay, axis=0)
    climb_rows = climb.T
    total = climb[-1]
    entering = jnp.where(opened[:, None], jnp.exp(climb), 0.0)
    leaving = jnp.where(tail_same[:, None], jnp.exp(total[None, :] - climb), 0.0)
    masks = [
        jnp.where(
            allowed,
            jnp.exp(jnp.minimum(climb[:, h : h + 1] - climb_rows[h : h + 1, :], 0.0)),
            0.0,
        )
        for h in range(heads)
    ]
    frequency = jnp.exp(-math.log(10000.0) * jnp.arange(dk // 2, dtype=f32) / (dk // 2))
    angles = positions.astype(f32)[:, None] * frequency[None, :]
    cosine, sine = jnp.cos(angles), jnp.sin(angles)

    wide = tokens.astype(f32)
    xhat1, inverse1 = norm_stats(wide)
    normed1 = (xhat1 * norm1_gain + norm1_bias).astype(bf16)
    keys, values, queries, gates, exits = [], [], [], [], []
    value_parts = [value_weight[:, h * dv : (h + 1) * dv] for h in range(heads)]
    gate_parts = [gate_weight[:, h * dv : (h + 1) * dv] for h in range(heads)]
    for h in range(heads):
        rows_k = dot(normed1, key_weight[:, h * dk : (h + 1) * dk])
        key = (rotate(rows_k, cosine, sine) * key_scale).astype(bf16)
        keys.append(key)
        values.append(dot(normed1, value_parts[h]).astype(bf16))
        exits.append((key.astype(f32) * leaving[:, h : h + 1]).astype(bf16))
    states = jnp.concatenate([token_sum(exits[h], values[h]) for h in range(heads)], axis=0)
    pieces = states.astype(bf16).reshape(blocks, heads * dk // blocks, dv)
    marks = jnp.concatenate([part for part in split3(total)])
    marks = jnp.broadcast_to(
        jnp.pad(marks, (0, 128 - 3 * heads - dv % 128))[None, None, :],
        (blocks, pieces.shape[1], 128 - dv % 128),
    )
    arrived = lax.all_to_all(jnp.concatenate([pieces, marks], axis=2), SEQ, 0, 0, tiled=True)
    tags = arrived[:, 0, dv : dv + 3 * heads].astype(f32)
    log_totals = tags[:, :heads] + tags[:, heads : 2 * heads] + tags[:, 2 * heads :]
    piece_head = seq_at // (blocks // heads)
    carried = block_weights(log_totals, starts, rows, piece_head).astype(bf16)
    summed = lax.dot_general(
        carried, arrived[:, :, :dv], (((1,), (0,)), ((), ())), preferred_element_type=f32
    ).astype(bf16)
    incoming = lax.all_to_all(summed, SEQ, 0, 0, tiled=True).reshape(heads * dk, dv)
    incoming, other_cot = lax.optimization_barrier((incoming, other_cot))

    mixed, ghats, ginvs, weights = [], [], [], []
    branch = None
    output_parts = [output_weight[h * dv : (h + 1) * dv] for h in range(heads)]
    for h in range(heads):
        rows_q = dot(normed1, query_weight[:, h * dk : (h + 1) * dk])
        query = rotate(rows_q, cosine, sine).astype(bf16)
        queries.append(query)
        gates.append(dot(normed1, gate_parts[h]))
        weight = (row_times(query, keys[h]) * masks[h]).astype(bf16)
        weights.append(weight)
        retained = dot(weight, values[h])
        retained = retained + entering[:, h : h + 1] * dot(query, incoming[h * dk : (h + 1) * dk])
        ghat, ginv = norm_stats(retained)
        ghats.append(ghat)
        ginvs.append(ginv)
        mix = (jax.nn.silu(gates[h]) * ghat).astype(bf16)
        mixed.append(mix)
        part = dot(mix, output_parts[h])
        branch = part if branch is None else branch + part
    branch = branch.astype(bf16)
    resid = wide + branch.astype(f32) + swap_heads(branch).astype(f32)

    xhat2, inverse2 = norm_stats(resid)
    normed2 = (xhat2 * norm2_gain + norm2_bias).astype(bf16)
    gate_ff = dot(normed2, ffn_gate)
    up_ff = dot(normed2, ffn_up)
    cdf = 0.5 * (1.0 + lax.erf(gate_ff * (0.5**0.5)))
    gelu = gate_ff * cdf
    hidden = (gelu * up_ff).astype(bf16)
    ffn_out = dot(hidden, ffn_down).astype(bf16)
    low, high = ffn_out[:, :half], ffn_out[:, half:]
    arrived_out = swap_heads(jnp.where(first_head, high, low))
    own_resid = jnp.where(first_head, resid[:, :half], resid[:, half:])

    cot = jnp.concatenate(
        [
            jnp.where(first_head, cotangent, other_cot),
            jnp.where(first_head, other_cot, cotangent),
        ],
        axis=1,
    )
    hidden_grad = row_times(cot, ffn_down)
    pdf = (1.0 / math.sqrt(2.0 * math.pi)) * jnp.exp(-0.5 * gate_ff * gate_ff)
    gate_ff_grad = (hidden_grad * up_ff * (cdf + gate_ff * pdf)).astype(bf16)
    up_ff_grad = (hidden_grad * gelu).astype(bf16)
    normed2_part = (row_times(gate_ff_grad, ffn_gate) + row_times(up_ff_grad, ffn_up)).astype(bf16)
    normed2_grad = normed2_part.astype(f32) + swap_heads(normed2_part).astype(f32)
    gain2_grad = jnp.sum(normed2_grad * xhat2, axis=0)
    bias2_grad = jnp.sum(normed2_grad, axis=0)
    resid_grad = cot.astype(f32) + norm_back(xhat2, inverse2, normed2_grad * norm2_gain)
    branch_grad = resid_grad.astype(bf16)

    ffn_sum = exchange_sum(
        [
            token_sum(normed2, gate_ff_grad),
            token_sum(normed2, up_ff_grad),
            token_sum(cot, hidden),
        ]
    )

    gate_grads, retained_grads, state_parts = [], [], []
    for h in range(heads):
        mixed_grad = row_times(branch_grad, output_parts[h])
        sig = jax.nn.sigmoid(gates[h])
        gate_grads.append(
            (mixed_grad * ghats[h] * (sig * (1.0 + gates[h] * (1.0 - sig)))).astype(bf16)
        )
        retained_grad = norm_back(ghats[h], ginvs[h], mixed_grad * (gates[h] * sig)).astype(bf16)
        retained_grads.append(retained_grad)
        scaled = (queries[h].astype(f32) * entering[:, h : h + 1]).astype(bf16)
        state_parts.append(token_sum(scaled, retained_grad))
    pieces = jnp.concatenate(state_parts, axis=0).astype(bf16)
    pieces = pieces.reshape(blocks, heads * dk // blocks, dv)
    arrived_back = lax.all_to_all(pieces, SEQ, 0, 0, tiled=True)
    summed_back = lax.dot_general(
        carried, arrived_back, (((0,), (0,)), ((), ())), preferred_element_type=f32
    ).astype(bf16)
    outgoing = lax.all_to_all(summed_back, SEQ, 0, 0, tiled=True).reshape(heads * dk, dv)

    gate_grad = jnp.concatenate(gate_grads, axis=1)
    branch_sum = exchange_sum(
        [
            token_sum(normed1, gate_grad),
            token_sum(branch_grad, jnp.concatenate(mixed, axis=1)),
        ]
    )
    outgoing, arrived_out = lax.optimization_barrier((outgoing, arrived_out))
    output = (
        own_resid + (jnp.where(first_head, low, high).astype(f32) + arrived_out.astype(f32))
    ).astype(bf16)

    query_grads, key_grads, value_grads = [], [], []
    for h in range(heads):
        rg = retained_grads[h]
        out_state = outgoing[h * dk : (h + 1) * dk]
        in_state = incoming[h * dk : (h + 1) * dk]
        score_grad = (row_times(rg, values[h]) * masks[h]).astype(bf16)
        query_rot = dot(score_grad, keys[h]) + entering[:, h : h + 1] * row_times(rg, in_state)
        key_rot = token_sum(score_grad, queries[h]) + leaving[:, h : h + 1] * row_times(
            values[h], out_state
        )
        value_grad = token_sum(weights[h], rg) + leaving[:, h : h + 1] * dot(keys[h], out_state)
        query_grads.append(rotate(query_rot, cosine, -sine).astype(bf16))
        key_grads.append((rotate(key_rot, cosine, -sine) * key_scale).astype(bf16))
        value_grads.append(value_grad.astype(bf16))
    normed1_part = None
    for h in range(heads):
        for grad, weight in (
            (query_grads[h], query_weight[:, h * dk : (h + 1) * dk]),
            (key_grads[h], key_weight[:, h * dk : (h + 1) * dk]),
            (value_grads[h], value_parts[h]),
            (gate_grads[h], gate_parts[h]),
        ):
            part = row_times(grad, weight)
            normed1_part = part if normed1_part is None else normed1_part + part
    normed1_part = normed1_part.astype(bf16)
    low, high = normed1_part[:, :half], normed1_part[:, half:]
    arrived_grad = swap_heads(jnp.where(first_head, high, low))
    normed1_grad = jnp.where(first_head, low, high).astype(f32) + arrived_grad.astype(f32)
    own_hat = jnp.where(first_head, xhat1[:, :half], xhat1[:, half:])
    own_gain = jnp.where(first_head, norm1_gain[:half], norm1_gain[half:])
    scaled_grad = normed1_grad * own_gain
    sums = jnp.stack([jnp.sum(scaled_grad, axis=1), jnp.sum(scaled_grad * own_hat, axis=1)])
    sums = (sums + swap_heads(sums)) * (1.0 / width)
    own_back = inverse1 * (scaled_grad - sums[0][:, None] - own_hat * sums[1][:, None])
    own_resid_grad = jnp.where(first_head, resid_grad[:, :half], resid_grad[:, half:])
    input_grad = (own_resid_grad + own_back).astype(bf16)
    own_norm1 = jnp.stack([jnp.sum(normed1_grad * own_hat, axis=0), jnp.sum(normed1_grad, axis=0)])
    other_norm1 = swap_heads(own_norm1)
    norm1_grads = jnp.concatenate(
        [
            jnp.where(first_head, own_norm1, other_norm1),
            jnp.where(first_head, other_norm1, own_norm1),
        ],
        axis=1,
    )
    vectors = jnp.concatenate([norm1_grads, gain2_grad[None], bias2_grad[None]], axis=0)
    vector_high = vectors.astype(bf16)
    vector_low = (vectors - vector_high.astype(f32)).astype(bf16)

    query_grad = jnp.concatenate(query_grads, axis=1)
    key_grad = jnp.concatenate(key_grads, axis=1)
    value_grad = jnp.concatenate(value_grads, axis=1)
    marks = jnp.concatenate([vector_high, vector_low], axis=0).T
    spare = 128 - value_grad.shape[1] % 128
    value_part = jnp.pad(token_sum(normed1, value_grad), ((0, 0), (0, spare)))
    value_part = value_part.astype(bf16) + jnp.pad(
        marks, ((0, 0), (value_grad.shape[1], spare - marks.shape[1]))
    )
    projection_sum = exchange_sum(
        [
            jnp.concatenate(
                [
                    token_sum(normed1, query_grad).astype(bf16),
                    token_sum(normed1, key_grad).astype(bf16),
                    value_part,
                ],
                axis=1,
            )
        ]
    )[:, 0]
    query_out = projection_sum[:, : heads * dk]
    key_out = projection_sum[:, heads * dk : 2 * heads * dk]
    value_out = projection_sum[:, 2 * heads * dk : heads * (2 * dk + dv)]
    marks_out = projection_sum[:, heads * (2 * dk + dv) :]
    vector_out = marks_out[:, :4] + marks_out[:, 4:8]
    gate_out, output_out = branch_sum[:, 0], branch_sum[:, 1].T
    ffn_gate_out, ffn_up_out, ffn_down_out = ffn_sum[:, 0], ffn_sum[:, 1], ffn_sum[:, 2].T
    return (
        output,
        input_grad,
        vector_out[:, 0],
        vector_out[:, 1],
        query_out,
        key_out,
        value_out,
        gate_out,
        output_out,
        vector_out[:, 2],
        vector_out[:, 3],
        ffn_gate_out,
        ffn_up_out,
        ffn_down_out,
    )


def solution(mesh):
    fine = Mesh(mesh.devices.reshape(4, 2, 4, 2, 2), SEQ + (HEAD,))
    return jax.shard_map(
        local,
        mesh=fine,
        in_specs=(
            P(SEQ, None),
            P(SEQ, HEAD),
            P(),
            P(),
            P(),
            P(None, HEAD),
            P(None, HEAD),
            P(None, HEAD),
            P(None, HEAD),
            P(HEAD, None),
            P(),
            P(),
            P(None, HEAD),
            P(None, HEAD),
            P(HEAD, None),
            P(SEQ, HEAD),
        ),
        out_specs=(
            P(SEQ, HEAD),
            P(SEQ, HEAD),
            P(SEQ),
            P(SEQ),
            P(SEQ, HEAD),
            P(SEQ, HEAD),
            P(SEQ, HEAD),
            P(SEQ, HEAD),
            P(HEAD, SEQ),
            P(SEQ),
            P(SEQ),
            P(SEQ, HEAD),
            P(SEQ, HEAD),
            P(HEAD, SEQ),
        ),
        check_vma=False,
    )
```

```python
import math

import jax
import jax.numpy as jnp
from jax import lax
from jax.experimental import pallas as pl
from jax.experimental.pallas import tpu as pltpu
from jax.sharding import Mesh, PartitionSpec as P

eps_norm = 1e-05
bf16 = jnp.bfloat16
f32 = jnp.float32
SEQ = ("y", "zlo", "x", "core")
STAGES = ("core", "x", "y", "zlo")
HEAD = "zhi"
SWAP = [(0, 1), (1, 0)]


def dot(left, right):
    return lax.dot_general(left, right, (((1,), (0,)), ((), ())), preferred_element_type=f32)


def token_sum(left, right):
    return lax.dot_general(left, right, (((0,), (0,)), ((), ())), preferred_element_type=f32)


def row_times(left, right):
    return lax.dot_general(left, right, (((1,), (1,)), ((), ())), preferred_element_type=f32)


def norm_stats(values):
    average = jnp.mean(values, axis=-1, keepdims=True)
    centred = values - average
    variance = jnp.mean(centred * centred, axis=-1, keepdims=True)
    inverse = lax.rsqrt(variance + eps_norm)
    return centred * inverse, inverse


def norm_back(xhat, inverse, grad):
    first = jnp.mean(grad, axis=-1, keepdims=True)
    second = jnp.mean(grad * xhat, axis=-1, keepdims=True)
    return inverse * (grad - first - xhat * second)


def swap_heads(array):
    return lax.ppermute(array, HEAD, SWAP)


def rotate(vectors, cosine, sine):
    upper, lower = vectors[:, : cosine.shape[1]], vectors[:, cosine.shape[1] :]
    return jnp.concatenate([upper * cosine - lower * sine, lower * cosine + upper * sine], axis=1)


def split3(values):
    first = values.astype(bf16)
    rest = values - first.astype(f32)
    second = rest.astype(bf16)
    third = (rest - second.astype(f32)).astype(bf16)
    return first, second, third


def own_rows(array, at):
    count = array.shape[0] // 2
    return lax.dynamic_slice_in_dim(array, at * count, count, 0)


def own_features(array, at):
    count = array.shape[1] // 2
    return lax.dynamic_slice_in_dim(array, at * count, count, 1)


def in_order(first, own, other, axis):
    return jnp.concatenate([jnp.where(first, own, other), jnp.where(first, other, own)], axis=axis)


def stacked_kernel(count, *refs):
    out_ref = refs[-1]
    for i in range(count):
        left, right = refs[2 * i], refs[2 * i + 1]
        grad = token_sum(left[...], right[...]).astype(bf16)
        for low in range(2):
            for x in range(4):
                for core in range(2):
                    at = ((low * 4 + x) * 2 + core) * 16
                    out_ref[core, x, 0, low, i] = grad[at : at + 16]


def stacked_grads(pairs):
    width = pairs[0][0].shape[1]
    columns = pairs[0][1].shape[1]
    count = len(pairs)
    steps = 4
    in_specs, operands, macs, moved = [], [], 0, 0
    for left, right in pairs:
        tokens = left.shape[0]
        in_specs.append(pl.BlockSpec((tokens, width // steps), lambda i: (0, i)))
        in_specs.append(pl.BlockSpec((tokens, columns), lambda i: (0, 0)))
        operands += [left, right]
        macs += tokens * width * columns
        moved += 2 * (tokens * width + tokens * columns + width * columns)
    out = pl.pallas_call(
        lambda *refs: stacked_kernel(count, *refs),
        grid=(steps,),
        in_specs=in_specs,
        out_specs=pl.BlockSpec(
            (2, 4, 1, 2, count, 16, columns), lambda i: (0, 0, i, 0, 0, 0, 0)
        ),
        out_shape=jax.ShapeDtypeStruct((2, 4, 4, 2, count, 16, columns), bf16),
        compiler_params=pltpu.CompilerParams(
            dimension_semantics=("arbitrary",), vmem_limit_bytes=48 * 2**20
        ),
        cost_estimate=pl.CostEstimate(flops=2 * macs, bytes_accessed=moved, transcendentals=0),
    )(*operands)
    return out.reshape(-1, columns)


def scatter_sum(stacked, axis):
    return lax.psum_scatter(stacked, axis, scatter_dimension=0, tiled=True)


def tie(*arrays):
    return lax.optimization_barrier(arrays)


def side_kernel(x_ref, query_ref, key_ref, value_ref, marks_ref, out_ref):
    left = x_ref[...]
    n = query_ref.shape[1]
    out_ref[:, :n] = token_sum(left, query_ref[...]).astype(bf16)
    out_ref[:, n : 2 * n] = token_sum(left, key_ref[...]).astype(bf16)
    value = token_sum(left, value_ref[...]).astype(bf16)
    full = value.shape[1] - 128
    out_ref[:, 2 * n : 2 * n + full] = value[:, :full]
    out_ref[:, 2 * n + full :] = value[:, full:] + marks_ref[...]


def side_grads(left, query, key, value, marks):
    tokens, width = left.shape
    steps = 4
    columns = query.shape[1] + key.shape[1] + value.shape[1]
    return pl.pallas_call(
        side_kernel,
        grid=(steps,),
        in_specs=[
            pl.BlockSpec((tokens, width // steps), lambda i: (0, i)),
            pl.BlockSpec(query.shape, lambda i: (0, 0)),
            pl.BlockSpec(key.shape, lambda i: (0, 0)),
            pl.BlockSpec(value.shape, lambda i: (0, 0)),
            pl.BlockSpec((width // steps, 128), lambda i: (i, 0)),
        ],
        out_specs=pl.BlockSpec((width // steps, columns), lambda i: (i, 0)),
        out_shape=jax.ShapeDtypeStruct((width, columns), bf16),
        compiler_params=pltpu.CompilerParams(
            dimension_semantics=("arbitrary",), vmem_limit_bytes=48 * 2**20
        ),
        cost_estimate=pl.CostEstimate(
            flops=2 * tokens * width * columns,
            bytes_accessed=2 * (tokens * (width + columns) + width * columns),
            transcendentals=0,
        ),
    )(left, query, key, value, marks)


def block_weights(log_totals, starts, row_count, head):
    blocks = log_totals.shape[0]
    begin = jnp.arange(blocks, dtype=jnp.int32) * row_count
    has_start = jnp.any(
        (starts[None, :] >= begin[:, None]) & (starts[None, :] < begin[:, None] + row_count), axis=1
    )
    own = jnp.where(head == 0, log_totals[:, 0], log_totals[:, 1])
    index = jnp.arange(blocks, dtype=jnp.int32)
    inner = (index[None, :, None] < index[None, None, :]) & (
        index[None, None, :] < index[:, None, None]
    )
    logs = jnp.sum(jnp.where(inner, own[None, None, :], 0.0), axis=2)
    broken = jnp.any(inner & has_start[None, None, :], axis=2)
    later = index[:, None] > index[None, :]
    return jnp.where(later & ~broken, jnp.exp(logs), 0.0)


def local(
    tokens,
    log_decay,
    starts,
    norm1_gain,
    norm1_bias,
    query_weight,
    key_weight,
    value_weight,
    gate_weight,
    output_weight,
    norm2_gain,
    norm2_bias,
    ffn_gate,
    ffn_up,
    ffn_down,
    cotangent,
):
    rows, width = tokens.shape
    heads = log_decay.shape[1]
    dk = query_weight.shape[1] // heads
    dv = value_weight.shape[1] // heads
    half = width // 2
    blocks = lax.axis_size(SEQ)
    seq_at = lax.axis_index(SEQ)
    head_at = lax.axis_index(HEAD)
    first_head = head_at == 0
    block_start = seq_at * rows
    key_scale = dk ** (-0.5)

    other_cot = swap_heads(own_rows(cotangent, 1 - head_at))
    slices = width // blocks
    place = 0
    for axis in ("core", "y", "x", "zlo"):
        place = place * lax.axis_size(axis) + lax.axis_index(axis)
    mine = jnp.stack(
        [
            lax.dynamic_slice_in_dim(ffn_gate, place * slices, slices, 0),
            lax.dynamic_slice_in_dim(ffn_up, place * slices, slices, 0),
            lax.dynamic_slice_in_dim(ffn_down, place * slices, slices, 1).T,
        ]
    )
    gathered = swap_heads(mine)
    low_at = lax.axis_index("zlo") == 0
    gathered = in_order(low_at, gathered[None], lax.ppermute(gathered, "zlo", SWAP)[None], 0)
    gathered = lax.all_gather(gathered, ("y", "x"))
    gathered = lax.all_gather(gathered, "core")
    other_gate, other_up, other_down = (
        gathered[:, :, :, i].reshape(width, -1) for i in range(3)
    )

    positions = block_start + jnp.arange(rows, dtype=jnp.int32)
    started = starts[None, :] <= positions[:, None]
    doc_ids = jnp.sum(started.astype(jnp.int32), axis=1)
    inside = jnp.logical_and(starts[None, :] >= block_start, started)
    opened = jnp.sum(inside.astype(jnp.int32), axis=1) == 0
    tail_same = doc_ids == doc_ids[-1]
    allowed = (positions[:, None] >= positions[None, :]) & (doc_ids[:, None] == doc_ids[None, :])
    climb = jnp.cumsum(log_decay, axis=0)
    climb_rows = climb.T
    total = climb[-1]
    entering = jnp.where(opened[:, None], jnp.exp(climb), 0.0)
    leaving = jnp.where(tail_same[:, None], jnp.exp(total[None, :] - climb), 0.0)
    masks = [
        jnp.where(
            allowed,
            jnp.exp(jnp.minimum(climb[:, h : h + 1] - climb_rows[h : h + 1, :], 0.0)),
            0.0,
        )
        for h in range(heads)
    ]
    frequency = jnp.exp(-math.log(10000.0) * jnp.arange(dk // 2, dtype=f32) / (dk // 2))
    angles = positions.astype(f32)[:, None] * frequency[None, :]
    cosine, sine = jnp.cos(angles), jnp.sin(angles)

    wide = tokens.astype(f32)
    xhat1, inverse1 = norm_stats(wide)
    normed1 = (xhat1 * norm1_gain + norm1_bias).astype(bf16)
    keys, values, queries, gates, exits = [], [], [], [], []
    value_parts = [value_weight[:, h * dv : (h + 1) * dv] for h in range(heads)]
    gate_parts = [gate_weight[:, h * dv : (h + 1) * dv] for h in range(heads)]
    for h in range(heads):
        rows_k = dot(normed1, key_weight[:, h * dk : (h + 1) * dk])
        key = (rotate(rows_k, cosine, sine) * key_scale).astype(bf16)
        keys.append(key)
        values.append(dot(normed1, value_parts[h]).astype(bf16))
        exits.append((key.astype(f32) * leaving[:, h : h + 1]).astype(bf16))
    states = jnp.concatenate([token_sum(exits[h], values[h]) for h in range(heads)], axis=0)
    pieces = states.astype(bf16).reshape(blocks, heads * dk // blocks, dv)
    marks = jnp.concatenate([part for part in split3(total)])
    marks = jnp.broadcast_to(
        jnp.pad(marks, (0, 128 - 3 * heads - dv % 128))[None, None, :],
        (blocks, pieces.shape[1], 128 - dv % 128),
    )
    arrived = lax.all_to_all(jnp.concatenate([pieces, marks], axis=2), SEQ, 0, 0, tiled=True)
    tags = arrived[:, 0, dv : dv + 3 * heads].astype(f32)
    log_totals = tags[:, :heads] + tags[:, heads : 2 * heads] + tags[:, 2 * heads :]
    piece_head = seq_at // (blocks // heads)
    carried = block_weights(log_totals, starts, rows, piece_head).astype(bf16)
    summed = lax.dot_general(
        carried, arrived[:, :, :dv], (((1,), (0,)), ((), ())), preferred_element_type=f32
    ).astype(bf16)
    incoming = lax.all_to_all(summed, SEQ, 0, 0, tiled=True).reshape(heads * dk, dv)
    incoming, other_cot = lax.optimization_barrier((incoming, other_cot))

    mixed, ghats, ginvs, weights = [], [], [], []
    output_parts = [output_weight[h * dv : (h + 1) * dv] for h in range(heads)]
    for h in range(heads):
        rows_q = dot(normed1, query_weight[:, h * dk : (h + 1) * dk])
        query = rotate(rows_q, cosine, sine).astype(bf16)
        queries.append(query)
        gates.append(dot(normed1, gate_parts[h]))
        weight = (row_times(query, keys[h]) * masks[h]).astype(bf16)
        weights.append(weight)
        retained = dot(weight, values[h])
        retained = retained + entering[:, h : h + 1] * dot(query, incoming[h * dk : (h + 1) * dk])
        ghat, ginv = norm_stats(retained)
        ghats.append(ghat)
        ginvs.append(ginv)
        mix = (jax.nn.silu(gates[h]) * ghat).astype(bf16)
        mixed.append(mix)
    mixed = jnp.concatenate(mixed, axis=1)
    sent_branch = dot(own_rows(mixed, 1 - head_at), output_weight).astype(bf16)
    kept_branch = dot(own_rows(mixed, head_at), output_weight)
    got_branch = swap_heads(sent_branch)
    resid = own_rows(tokens, head_at).astype(f32) + kept_branch + got_branch.astype(f32)

    xhat2, inverse2 = norm_stats(resid)
    normed2 = (xhat2 * norm2_gain + norm2_bias).astype(bf16)
    cot = in_order(first_head, own_rows(cotangent, head_at), other_cot, 1)
    hiddens, gate_ff_grads, up_ff_grads = [], [], []
    for side in range(2):
        gate_ff = dot(normed2, (ffn_gate, other_gate)[side])
        up_ff = dot(normed2, (ffn_up, other_up)[side])
        hidden_grad = dot(cot, other_down) if side else row_times(cot, ffn_down)
        cdf = 0.5 * (1.0 + lax.erf(gate_ff * (0.5**0.5)))
        gelu = gate_ff * cdf
        pdf = (1.0 / math.sqrt(2.0 * math.pi)) * jnp.exp(-0.5 * gate_ff * gate_ff)
        hiddens.append((gelu * up_ff).astype(bf16))
        gate_ff_grads.append((hidden_grad * up_ff * (cdf + gate_ff * pdf)).astype(bf16))
        up_ff_grads.append((hidden_grad * gelu).astype(bf16))
    normed2_grad = (row_times(gate_ff_grads[0], ffn_gate) + row_times(up_ff_grads[0], ffn_up)) + (
        row_times(gate_ff_grads[1], other_gate) + row_times(up_ff_grads[1], other_up)
    )
    norm2_grads = jnp.stack([jnp.sum(normed2_grad * xhat2, axis=0), jnp.sum(normed2_grad, axis=0)])
    resid_grad = cot.astype(f32) + norm_back(xhat2, inverse2, normed2_grad * norm2_gain)
    own_branch_grad = resid_grad.astype(bf16)
    out_rows = resid + dot(hiddens[0], ffn_down) + row_times(hiddens[1], other_down)
    out_rows = out_rows.astype(bf16)
    got_out = swap_heads(own_features(out_rows, 1 - head_at))
    own_branch_grad, gate_ff_grads[0] = tie(own_branch_grad, gate_ff_grads[0])
    other_branch_grad = swap_heads(own_branch_grad)
    ffn_stack = stacked_grads(
        [
            (left, right)
            for side in range(2)
            for left, right in (
                (normed2, gate_ff_grads[side]),
                (normed2, up_ff_grads[side]),
                (cot, hiddens[side]),
            )
        ]
    )
    ffn_sums = scatter_sum(ffn_stack, "core")
    other_branch_grad, ffn_sums = tie(other_branch_grad, ffn_sums)
    ffn_sums = scatter_sum(ffn_sums, "x")
    branch_grad = in_order(first_head, own_branch_grad, other_branch_grad, 0)

    gate_grads, retained_grads, state_parts = [], [], []
    for h in range(heads):
        mixed_grad = row_times(branch_grad, output_parts[h])
        sig = jax.nn.sigmoid(gates[h])
        gate_grads.append(
            (mixed_grad * ghats[h] * (sig * (1.0 + gates[h] * (1.0 - sig)))).astype(bf16)
        )
        retained_grad = norm_back(ghats[h], ginvs[h], mixed_grad * (gates[h] * sig)).astype(bf16)
        retained_grads.append(retained_grad)
        scaled = (queries[h].astype(f32) * entering[:, h : h + 1]).astype(bf16)
        state_parts.append(token_sum(scaled, retained_grad))
    pieces = jnp.concatenate(state_parts, axis=0).astype(bf16)
    pieces = pieces.reshape(blocks, heads * dk // blocks, dv)
    arrived_back = lax.all_to_all(pieces, SEQ, 0, 0, tiled=True)
    arrived_back, ffn_sums = tie(arrived_back, ffn_sums)
    ffn_sums = scatter_sum(ffn_sums, "y")
    summed_back = lax.dot_general(
        carried, arrived_back, (((0,), (0,)), ((), ())), preferred_element_type=f32
    ).astype(bf16)
    outgoing = lax.all_to_all(summed_back, SEQ, 0, 0, tiled=True).reshape(heads * dk, dv)

    gate_grad = jnp.concatenate(gate_grads, axis=1)
    branch_stack = stacked_grads([(normed1, gate_grad), (branch_grad, mixed)])
    branch_sum = scatter_sum(branch_stack, "core")
    outgoing, got_out, ffn_sums, branch_sum = tie(outgoing, got_out, ffn_sums, branch_sum)
    ffn_sums = scatter_sum(ffn_sums, "zlo").reshape(6, slices, -1)
    branch_sum = scatter_sum(branch_sum, "x")
    output = in_order(first_head, own_features(out_rows, head_at), got_out, 0)

    query_grads, key_grads, value_grads = [], [], []
    for h in range(heads):
        rg = retained_grads[h]
        out_state = outgoing[h * dk : (h + 1) * dk]
        in_state = incoming[h * dk : (h + 1) * dk]
        score_grad = (row_times(rg, values[h]) * masks[h]).astype(bf16)
        query_rot = dot(score_grad, keys[h]) + entering[:, h : h + 1] * row_times(rg, in_state)
        key_rot = token_sum(score_grad, queries[h]) + leaving[:, h : h + 1] * row_times(
            values[h], out_state
        )
        value_grad = token_sum(weights[h], rg) + leaving[:, h : h + 1] * dot(keys[h], out_state)
        query_grads.append(rotate(query_rot, cosine, -sine).astype(bf16))
        key_grads.append((rotate(key_rot, cosine, -sine) * key_scale).astype(bf16))
        value_grads.append(value_grad.astype(bf16))
    normed1_part = None
    for h in range(heads):
        for grad, weight in (
            (query_grads[h], query_weight[:, h * dk : (h + 1) * dk]),
            (key_grads[h], key_weight[:, h * dk : (h + 1) * dk]),
            (value_grads[h], value_parts[h]),
            (gate_grads[h], gate_parts[h]),
        ):
            part = row_times(grad, weight)
            normed1_part = part if normed1_part is None else normed1_part + part
    norm1_grads = jnp.stack([jnp.sum(normed1_part * xhat1, axis=0), jnp.sum(normed1_part, axis=0)])
    normed1_part, branch_sum, ffn_sums = tie(normed1_part.astype(bf16), branch_sum, ffn_sums)
    ffn_sum = ffn_sums[:3].astype(f32) + swap_heads(ffn_sums[3:]).astype(f32)
    branch_sum = scatter_sum(branch_sum, "y")
    low, high = normed1_part[:, :half], normed1_part[:, half:]
    arrived_grad = swap_heads(jnp.where(first_head, high, low))
    arrived_grad, branch_sum = tie(arrived_grad, branch_sum)
    branch_sum = scatter_sum(branch_sum, "zlo").reshape(2, slices, -1).astype(f32)
    normed1_grad = jnp.where(first_head, low, high).astype(f32) + arrived_grad.astype(f32)
    own_hat = jnp.where(first_head, xhat1[:, :half], xhat1[:, half:])
    own_gain = jnp.where(first_head, norm1_gain[:half], norm1_gain[half:])
    scaled_grad = normed1_grad * own_gain
    sums = jnp.stack([jnp.sum(scaled_grad, axis=1), jnp.sum(scaled_grad * own_hat, axis=1)])
    sums = (sums + swap_heads(sums)) * (1.0 / width)
    own_back = inverse1 * (scaled_grad - sums[0][:, None] - own_hat * sums[1][:, None])
    own_resid_grad = own_features(branch_grad, head_at).astype(f32)
    input_grad = (own_resid_grad + own_back).astype(bf16)
    vectors = jnp.concatenate([norm1_grads, norm2_grads], axis=0)
    vector_high = vectors.astype(bf16)
    vector_low = (vectors - vector_high.astype(f32)).astype(bf16)

    query_grad = jnp.concatenate(query_grads, axis=1)
    key_grad = jnp.concatenate(key_grads, axis=1)
    value_grad = jnp.concatenate(value_grads, axis=1)
    marks = jnp.concatenate([vector_high, vector_low], axis=0).T
    spare = 128 - value_grad.shape[1] % 128
    marks = jnp.pad(marks, ((0, 0), (128 - spare, spare - marks.shape[1])))
    value_grad = jnp.pad(value_grad, ((0, 0), (0, spare)))
    projections = side_grads(normed1, query_grad, key_grad, value_grad, marks)
    shares = lax.all_to_all(
        projections.reshape(blocks, slices, -1), SEQ, 0, 0, tiled=True
    )
    projection_sum = jnp.sum(shares.astype(f32), axis=0)
    query_out = projection_sum[:, : heads * dk]
    key_out = projection_sum[:, heads * dk : 2 * heads * dk]
    value_out = projection_sum[:, 2 * heads * dk : heads * (2 * dk + dv)]
    marks_out = projection_sum[:, heads * (2 * dk + dv) :]
    vector_out = marks_out[:, :4] + marks_out[:, 4:8]
    vector_out = vector_out + swap_heads(vector_out)
    gate_out, output_out = branch_sum[0], branch_sum[1].T
    ffn_gate_out, ffn_up_out, ffn_down_out = ffn_sum[0], ffn_sum[1], ffn_sum[2].T
    return (
        output,
        input_grad,
        vector_out[:, 0],
        vector_out[:, 1],
        query_out,
        key_out,
        value_out,
        gate_out,
        output_out,
        vector_out[:, 2],
        vector_out[:, 3],
        ffn_gate_out,
        ffn_up_out,
        ffn_down_out,
    )


def solution(mesh):
    fine = Mesh(mesh.devices.reshape(4, 2, 4, 2, 2), SEQ + (HEAD,))
    return jax.shard_map(
        local,
        mesh=fine,
        in_specs=(
            P(SEQ, None),
            P(SEQ, HEAD),
            P(),
            P(),
            P(),
            P(None, HEAD),
            P(None, HEAD),
            P(None, HEAD),
            P(None, HEAD),
            P(HEAD, None),
            P(),
            P(),
            P(None, HEAD),
            P(None, HEAD),
            P(HEAD, None),
            P(SEQ, HEAD),
        ),
        out_specs=(
            P(SEQ, HEAD),
            P(SEQ, HEAD),
            P(SEQ),
            P(SEQ),
            P(SEQ, HEAD),
            P(SEQ, HEAD),
            P(SEQ, HEAD),
            P(SEQ, HEAD),
            P(HEAD, SEQ),
            P(SEQ),
            P(SEQ),
            P(SEQ, HEAD),
            P(SEQ, HEAD),
            P(HEAD, SEQ),
        ),
        check_vma=False,
    )
```
